32 devices in a mesh: dp: 2 (over y), expert: 16 (over z, x, core).
Axes of the slice: x: 2, y: 2, z: 4, core: 2. Of those that a mesh axis runs over, the one named last changes fastest.
Arguments:
- cache: bfloat16 [4, 64, 1152], P('dp'), may hold values from -6 to 6
- requests: int32 [2, 16, 2], P(None, 'expert'), may hold values from 0 to 3
- routes: int32 [4096, 1], P('expert'), may hold values from 0 to 15; in each aligned block of 256 rows (0 to 255, 256 to 511, ...) at most 20 rows name the same one
- combine_weight: float32 [4096, 1], P('expert'), may hold values from 0.2 to 1
- proj_weight: bfloat16 [1152, 2048], P('expert', 'dp'), may hold values from -1 to 1
- norm_gain: float32 [2048], replicated, may hold values from 0.5 to 1.5
- gate_weight: bfloat16 [16, 2048, 1408], P('expert', None, 'dp'), may hold values from -0.125 to 0.125
- up_weight: bfloat16 [16, 2048, 1408], P('expert', None, 'dp'), may hold values from -0.125 to 0.125
- down_weight: bfloat16 [16, 1408, 2048], P('expert', None, 'dp'), may hold values from -0.15625 to 0.15625
- cotangent: bfloat16 [4096, 2048], P('expert', 'dp'), may hold values from -6 to 6
Outputs:
- mixed: bfloat16 [4096, 2048], P('expert', 'dp')
- down_grad: bfloat16 [16, 1408, 2048], P('expert', None, 'dp')
The draws below stay inside these ranges and needn't reach their ends.
Inputs may be any that keep to these rules, and one draw needn't show every extreme that they name: `routes`: among the 256 tokens of one column no expert is named more than 20 times, and in every draw some column names some expert exactly 20 times.
All inputs are finite; a program needn't handle non-finite values.
Results may differ from the reference program's by a relative error of at most 0.012.
Values may be sent and summed in bfloat16 or wider, within the bound.
A program may use at most 64 MiB of HBM per device.

```python
import math
import jax
import jax.numpy as jnp
import numpy as np
from jax import lax

D = 2048
FF = 1408
FEAT = 1152
TOPK = 1
BLOCK = 64
FETCH = 2
EXPERTS = 16
CACHE_BLOCKS = 4
TOK_COL = 256
TOKENS = 4096
CAPC = 20
N_DP = 2
N_EXPERT = 16


def draw_proj_weight(key, part):
    column_pos = jnp.arange(D, dtype=jnp.float32) / (D - 1)
    values = jax.random.normal(key, (FEAT, D), jnp.float32)
    column_scale = 0.6 + 1.2 * column_pos
    return (values * column_scale[None, :] / jnp.sqrt(jnp.float32(FEAT))).astype(jnp.bfloat16)


def plant(result, stream_key, smallest, high):
    shape = result.shape
    place = [jax.random.randint(jax.random.fold_in(stream_key, axis), (), 0, shape[axis]) for axis in range(len(shape))]
    result = result.at[tuple(place)].set(smallest)
    longest = shape.index(max(shape))
    place[longest] = (place[longest] + 1) % shape[longest]
    return result.at[tuple(place)].set(high)


def levels(stream_key, dims, shards, least, high):
    def one(dim, blocks):
        steps = jax.random.uniform(jax.random.fold_in(jax.random.fold_in(stream_key, 6), dim), (blocks,), jnp.float32, least / len(shards), high / len(shards))
        return jnp.repeat(jnp.exp(steps), dims[dim] // blocks).reshape((-1,) + (1,) * (len(dims) - dim - 1))

    gain = one(*shards[0])
    for cut in shards[1:]:
        gain = gain * one(*cut)
    return gain


def rank_table(count, slope):
    weights = [(1 << 20) // math.isqrt(rank ** slope) + 1 for rank in range(1, count + 1)]
    width = 1 + sum(weights) // (1 << 30)
    return np.cumsum(np.array([max(1, weight // width) for weight in weights]))


def ranked_ids(stream_key, dims, number_of, skew):
    table = rank_table(number_of, skew)
    pick = jax.random.randint(jax.random.fold_in(stream_key, 1), dims, 0, int(table[number_of - 1]))
    rank = jnp.searchsorted(jnp.asarray(table, jnp.int32), pick, side="right")
    return jax.random.permutation(jax.random.fold_in(stream_key, 2), number_of)[rank].astype(jnp.int32)


def assign_block(stream_key, own, number, rows, number_of, top, limit, lean):
    sequence = jax.random.permutation(stream_key, number_of)
    heavy_load, usual = load_shares(number_of, rows * top, limit, lean, True), load_shares(number_of, rows * top, limit, lean, False)
    places = jnp.arange(number_of)

    def named(tallies, turn):
        used = int((tallies > 0).sum())
        fixed = max(1, used // 4)
        passed = fixed + (places - fixed + turn * (used - fixed)) % max(1, number_of - fixed)
        return jnp.zeros((number_of,), jnp.int32).at[sequence[jnp.where(places < fixed, places, passed)]].set(jnp.asarray(tallies, jnp.int32))

    tallies = jnp.where(number % 4 == 0, named(heavy_load, number // 4), named(usual, number - number // 4 - 1))
    mixed = jax.random.permutation(jax.random.fold_in(own, 3), number_of)
    donor, receiver = mixed[0:number_of // 2 * 2:2], mixed[1:number_of // 2 * 2:2]
    room = jnp.minimum(tallies[donor] - 1, limit - tallies[receiver]) // 2
    room = jnp.where((donor == sequence[0]) | (receiver == sequence[0]) | (tallies[receiver] == 0), 0, jnp.maximum(room, 0))
    passed = jax.random.randint(jax.random.fold_in(own, 4), (number_of // 2,), 0, 1 << 20) % (room + 1)
    tallies = tallies.at[donor].add(-passed).at[receiver].add(passed)
    members = jnp.searchsorted(jnp.cumsum(tallies), jnp.arange(rows * top), side="right").astype(jnp.int32)
    listing = members.reshape(top, rows).T
    listing = listing[jax.random.permutation(jax.random.fold_in(own, 1), rows)]
    turn = jax.random.randint(jax.random.fold_in(own, 2), (rows, 1), 0, top)
    return jnp.take_along_axis(listing, (jnp.arange(top)[None, :] + turn) % top, axis=1)


def load_shares(amount, total, limit, slope, full):
    loads = [(1 << 20) // math.isqrt(grade ** slope) + 1 for grade in range(1, amount + 1)]
    largest = limit if full else min(limit, max(-(-total // amount), total * loads[0] // sum(loads)))
    least = 1 if total - largest >= amount - 1 else 0
    given, rest = [largest] + [least] * (amount - 1), total - largest - least * (amount - 1)
    while rest > 0:
        candidates = [i for i in range(1, amount) if given[i] < largest] or [i for i in range(1, amount) if given[i] < limit]
        mass, left = sum([loads[i] for i in candidates]), rest
        for i in candidates:
            addition = min(limit - given[i], max(1, left * loads[i] // mass), rest)
            given[i] = given[i] + addition
            rest = rest - addition
    return np.array(given)


def centred(own_key, shape, width, limit, pieces=(), kind=jnp.bfloat16):
    array = width * jax.random.normal(own_key, shape, jnp.float32)
    if pieces:
        array = array * levels(own_key, shape, pieces, -0.22, 0.18)
    return jnp.clip(array, -limit, limit).astype(kind)


def setup_inputs(seed: int = 0) -> dict:
    key_of = jax.random.split(jax.random.key(seed), 11)
    cache = centred(key_of[0], (CACHE_BLOCKS, BLOCK, FEAT), 1.0, 6.0, ((0, 2),))
    requests = plant(ranked_ids(key_of[1], (N_DP, N_EXPERT, FETCH), CACHE_BLOCKS, 2), jax.random.fold_in(key_of[1], 3), 0, CACHE_BLOCKS - 1).astype(jnp.int32)
    routes_keys = jax.random.split(jax.random.fold_in(key_of[2], 1), TOKENS // TOK_COL)
    routes_turns = jax.random.permutation(jax.random.fold_in(key_of[2], 3), TOKENS // TOK_COL)
    routes = jax.vmap(lambda own, number: assign_block(jax.random.fold_in(key_of[2], 2), own, number, TOK_COL, EXPERTS, TOPK, CAPC, 1))(routes_keys, routes_turns).reshape((TOKENS, TOPK))
    combine_weight = jnp.clip(0.2 + 0.8 * jax.random.uniform(key_of[3], (TOKENS, TOPK), jnp.float32) ** levels(key_of[3], (TOKENS, TOPK), ((0, 16),), -0.2, 0.2), 0.2, 1.0)
    proj_weight = draw_proj_weight(jax.random.fold_in(key_of[10], 71), 0)
    norm_gain = jnp.clip(1.0 + 0.1 * jax.random.normal(key_of[5], (D,), jnp.float32), 0.5, 1.5)
    gate_weight = centred(key_of[6], (EXPERTS, D, FF), D ** -0.5, 0.125, ((0, 16), (2, 2)))
    up_weight = centred(key_of[7], (EXPERTS, D, FF), D ** -0.5, 0.125, ((0, 16), (2, 2)))
    down_weight = centred(key_of[8], (EXPERTS, FF, D), FF ** -0.5, 0.15625, ((0, 16), (2, 2)))
    cotangent = centred(key_of[9], (TOKENS, D), 1.0, 6.0, ((0, 16), (1, 2)))
    return {"cache": cache, "requests": requests, "routes": routes, "combine_weight": combine_weight, "proj_weight": proj_weight, "norm_gain": norm_gain, "gate_weight": gate_weight, "up_weight": up_weight, "down_weight": down_weight, "cotangent": cotangent}


def column_tokens(ids, cache, proj_weight, norm_gain):
    gathered = cache[ids].reshape(-1, cache.shape[2])
    projected = jnp.dot(gathered, proj_weight, preferred_element_type=jnp.float32).astype(jnp.bfloat16)
    values = projected.astype(jnp.float32)
    mean_square = lax.optimization_barrier(jnp.mean(values * values, axis=1))
    return (values * lax.rsqrt(mean_square + 1e-06)[:, None] * norm_gain[None, :]).astype(jnp.bfloat16)

def expert_step(operands):
    row_block, grad_rows, w_gate, w_up, w_down = operands
    gate_act = jnp.dot(row_block, w_gate, preferred_element_type=jnp.float32)
    up_act = jnp.dot(row_block, w_up, preferred_element_type=jnp.float32)
    hidden = (jax.nn.silu(gate_act) * up_act).astype(jnp.bfloat16)
    expert_out = jnp.dot(hidden, w_down, preferred_element_type=jnp.float32).astype(jnp.bfloat16)
    grad_block = jnp.dot(hidden.T, grad_rows, preferred_element_type=jnp.float32).astype(jnp.bfloat16)
    return (expert_out, grad_block)

def reference(cache, requests, routes, combine_weight, proj_weight, norm_gain, gate_weight, up_weight, down_weight, cotangent):
    request_ids = jnp.transpose(requests, (1, 0, 2)).reshape(N_EXPERT, -1).astype(jnp.int32)

    def one_column(ids):
        return column_tokens(ids, cache, proj_weight, norm_gain)
    normed = lax.map(one_column, request_ids).reshape(TOKENS, D)
    expert_id = routes[:, 0].reshape(N_EXPERT, TOK_COL).astype(jnp.int32)
    onehot = (expert_id[:, :, None] == jnp.arange(EXPERTS, dtype=jnp.int32)[None, None, :]).astype(jnp.int32)
    slot_rank = lax.optimization_barrier(jnp.sum((jnp.cumsum(onehot, axis=1) - 1) * onehot, axis=2))
    column_index = jnp.arange(N_EXPERT, dtype=jnp.int32)[:, None]
    position = ((expert_id * N_EXPERT + column_index) * CAPC + slot_rank).reshape(TOKENS).astype(jnp.int32)
    scaled_grad = (combine_weight * cotangent.astype(jnp.float32)).astype(jnp.bfloat16)
    slot_total = EXPERTS * N_EXPERT * CAPC
    inputs = jnp.zeros((slot_total, D), jnp.bfloat16).at[position].set(normed)
    grads_in = jnp.zeros((slot_total, D), jnp.bfloat16).at[position].set(scaled_grad)
    outputs, down_grad = lax.map(expert_step, (inputs.reshape(EXPERTS, N_EXPERT * CAPC, D), grads_in.reshape(EXPERTS, N_EXPERT * CAPC, D), gate_weight, up_weight, down_weight))
    expert_rows = outputs.reshape(slot_total, D)[position]
    mixed = (combine_weight * expert_rows.astype(jnp.float32)).astype(jnp.bfloat16)
    return (mixed, down_grad)
```

```python
import jax
import jax.numpy as jnp
from jax import lax
from jax.sharding import PartitionSpec as P

BF = jnp.bfloat16
F32 = jnp.float32


def dot(a, b, dims=((1,), (0,))):
    return lax.dot_general(a, b, (dims, ((), ())), preferred_element_type=F32)


def body(
    cache,
    requests,
    routes,
    combine_weight,
    proj_weight,
    norm_gain,
    gate_weight,
    up_weight,
    down_weight,
    cotangent,
):
    width = cotangent.shape[1]
    n_expert = lax.axis_size("expert")
    experts = n_expert * gate_weight.shape[0]
    block, feat = cache.shape[1:]

    feats = lax.all_gather(cache, "dp", axis=0, tiled=True).reshape(-1, feat)
    lanes = width // n_expert
    piece = lax.all_to_all(
        proj_weight.reshape(-1, n_expert, lanes), "expert", split_axis=1, concat_axis=0, tiled=True
    ).reshape(feat, lanes)
    part = dot(feats, piece).astype(BF)
    projected = lax.all_gather(part, ("dp", "expert"), axis=1, tiled=True)
    values = projected.astype(F32)
    mean_square = jnp.mean(values * values, axis=1)
    table = (values * lax.rsqrt(mean_square + 1e-06)[:, None] * norm_gain[None, :]).astype(BF)
    table_rows = table.shape[0]

    token_row = (
        requests.reshape(-1)[:, None] * block + jnp.arange(block, dtype=jnp.int32)[None, :]
    ).reshape(-1)
    tokens = token_row.shape[0]
    capacity = max(2, 5 * tokens // (4 * experts))
    expert_id = routes[:, 0]
    order = jnp.arange(tokens, dtype=jnp.int32)
    earlier = (expert_id[:, None] == expert_id[None, :]) & (order[None, :] < order[:, None])
    slot_rank = jnp.sum(earlier.astype(jnp.int32), axis=1)
    position = expert_id * capacity + slot_rank
    hit = jnp.arange(experts * capacity, dtype=jnp.int32)[:, None] == position[None, :]
    pick = hit.astype(BF)
    slot_row = jnp.sum(jnp.where(hit, token_row[None, :] + 1, 0), axis=1) - 1

    token_weight = combine_weight[:, 0]
    scaled_grad = (token_weight[:, None] * cotangent.astype(F32)).astype(BF)
    sent = dot(pick, scaled_grad).astype(BF).reshape(experts, capacity, width)
    grad_rows = lax.all_to_all(sent, "expert", split_axis=0, concat_axis=0, tiled=True)
    grad_rows = grad_rows.reshape(-1, width)
    rows = lax.all_to_all(
        slot_row.reshape(experts, capacity), "expert", split_axis=0, concat_axis=0, tiled=True
    ).reshape(-1)
    select = (rows[:, None] == jnp.arange(table_rows, dtype=jnp.int32)[None, :]).astype(BF)

    gate_act = dot(table, gate_weight[0])
    up_act = dot(table, up_weight[0])
    half = (jax.nn.silu(gate_act) * up_act).astype(BF)
    hidden = lax.all_gather(half, "dp", axis=1, tiled=True)
    out_rows = dot(hidden, down_weight[0]).astype(BF)
    sent_out = dot(select, out_rows).astype(BF).reshape(-1, capacity, width)
    hidden_rows = dot(select, hidden).astype(BF)
    down_grad = dot(hidden_rows, grad_rows, ((0,), (0,))).astype(BF)
    returned = lax.all_to_all(sent_out, "expert", split_axis=0, concat_axis=0, tiled=True)
    token_out = dot(pick, returned.reshape(experts * capacity, width), ((0,), (0,)))
    mixed = (token_weight[:, None] * token_out).astype(BF)
    return mixed, down_grad[None]


def solution(mesh):
    return jax.shard_map(
        body,
        mesh=mesh,
        in_specs=(
            P("dp", None, None),
            P(None, "expert", None),
            P("expert", None),
            P("expert", None),
            P("expert", "dp"),
            P(),
            P("expert", None, "dp"),
            P("expert", None, "dp"),
            P("expert", None, "dp"),
            P("expert", "dp"),
        ),
        out_specs=(P("expert", "dp"), P("expert", None, "dp")),
        check_vma=False,
    )
```

```python
import functools

import jax
import jax.numpy as jnp
from jax import lax
from jax.experimental import pallas as pl
from jax.experimental.pallas import tpu as pltpu
from jax.sharding import PartitionSpec as P

MESH = pl.DeviceIdType.MESH

BF = jnp.bfloat16
F32 = jnp.float32


def dot(a, b, dims=((1,), (0,))):
    return lax.dot_general(a, b, (dims, ((), ())), preferred_element_type=F32)


def loop(start, stop, step):
    def run(i, carry):
        step(i)
        return carry

    lax.fori_loop(start, stop, run, 0)


def remote(src, dst, send_sem, recv_sem, device):
    return pltpu.make_async_remote_copy(
        src_ref=src,
        dst_ref=dst,
        send_sem=send_sem,
        recv_sem=recv_sem,
        device_id=device,
        device_id_type=MESH,
    )


def table_kernel(
    n_dp,
    n_expert,
    feat_ref,
    proj_ref,
    rows_ref,
    tab_ref,
    got_ref,
    held,
    proj_send,
    proj_recv,
    row_send,
    row_recv,
    dp_send,
    dp_recv,
    far_send,
    far_recv,
    near_send,
    near_recv,
):
    y = lax.axis_index("dp")
    e = lax.axis_index("expert")
    groups = n_expert // n_dp
    near = 4 if n_expert % 4 == 0 else 1
    far = n_expert // near
    a, b = e // near, e % near
    n = n_dp * n_expert
    me = y * n_expert + e
    other = ((y + 1) % n_dp, e)

    barrier = pltpu.get_barrier_semaphore()

    def greet(i):
        t = (me + i) % n
        pl.semaphore_signal(
            barrier, inc=1, device_id=(t // n_expert, t % n_expert), device_id_type=MESH
        )

    loop(1, n, greet)
    pl.semaphore_wait(barrier, n - 1)

    mine = e // groups == y

    def send_proj(dy, dj):
        j = (e + dj) % groups
        return remote(
            proj_ref.at[j],
            held.at[e],
            proj_send.at[dy * groups + dj],
            proj_recv.at[e],
            ((y + dy) % n_dp, y * groups + j),
        )

    for dj in range(groups):
        for dy in range(n_dp):
            if dy == 0 and dj == 0:
                pl.when(jnp.logical_not(mine))(lambda: send_proj(0, 0).start())
            else:
                send_proj(dy, dj).start()

    @pl.when(mine)
    def _():
        held[e] = proj_ref[e % groups]

    got_ref[e] = rows_ref[e]

    def send_row(i):
        t = (e + i) % n_expert
        return remote(rows_ref.at[t], got_ref.at[e], row_send.at[i], row_recv.at[i], (y, t))

    loop(1, n_expert, lambda i: send_row(i).start())

    def await_proj(i):
        s = (e + i) % n_expert
        remote(proj_ref.at[0], held.at[s], proj_send.at[0], proj_recv.at[s], other).wait_recv()

    pl.when(jnp.logical_not(mine))(lambda: await_proj(0))
    loop(1, n_expert, await_proj)

    weight = held[...].reshape(-1, held.shape[2])
    part = jnp.dot(feat_ref[...], weight, preferred_element_type=jnp.float32)
    tab_ref[e, y] = part.astype(jnp.bfloat16)

    def over_dp(d, src):
        return remote(
            tab_ref.at[e, src],
            tab_ref.at[e, src],
            dp_send.at[d],
            dp_recv.at[d],
            ((y + d) % n_dp, e),
        )

    for d in range(1, n_dp):
        over_dp(d, y).start()
    for d in range(1, n_dp):
        over_dp(d, (y + n_dp - d) % n_dp).wait_recv()

    def to_far(d, block):
        return remote(
            tab_ref.at[block],
            tab_ref.at[block],
            far_send.at[d],
            far_recv.at[d],
            (y, (a + d) % far * near + b),
        )

    def to_near(d, c, block):
        return remote(
            tab_ref.at[block],
            tab_ref.at[block],
            near_send.at[d, c],
            near_recv.at[d, c],
            (y, a * near + (b + c) % near),
        )

    for d in range(1, far):
        to_far(d, e).start()
    for d in range(far):
        block = (a + far - d) % far * near + b
        if d:
            to_far(d, block).wait_recv()
        for c in range(1, near):
            to_near(d, c, block).start()
    for d in range(far):
        for c in range(1, near):
            to_near(d, c, (a + far - d) % far * near + (b + near - c) % near).wait_recv()

    def await_row(i):
        s = (e + n_expert - i) % n_expert
        remote(
            rows_ref.at[0], got_ref.at[s], row_send.at[i], row_recv.at[i], other
        ).wait_recv()

    loop(1, n_expert, await_row)
    pl.when(jnp.logical_not(mine))(lambda: send_proj(0, 0).wait_send())
    for dj in range(groups):
        for dy in range(n_dp):
            if dy or dj:
                send_proj(dy, dj).wait_send()
    loop(1, n_expert, lambda i: send_row(i).wait_send())
    for d in range(1, n_dp):
        over_dp(d, y).wait_send()
    for d in range(1, far):
        to_far(d, e).wait_send()
    for d in range(far):
        for c in range(1, near):
            to_near(d, c, (a + far - d) % far * near + b).wait_send()


def share_kernel(n_dp, half_ref, out_ref, send_sem, recv_sem):
    y = lax.axis_index("dp")
    e = lax.axis_index("expert")
    barrier = pltpu.get_barrier_semaphore()
    for d in range(1, n_dp):
        pl.semaphore_signal(
            barrier, inc=1, device_id=((y + d) % n_dp, e), device_id_type=MESH
        )
    pl.semaphore_wait(barrier, n_dp - 1)

    def send(d, src):
        return remote(
            half_ref, out_ref.at[src], send_sem.at[d], recv_sem.at[d], ((y + d) % n_dp, e)
        )

    for d in range(1, n_dp):
        send(d, y).start()
    out_ref[y] = half_ref[...]
    for d in range(1, n_dp):
        send(d, (y + n_dp - d) % n_dp).wait_recv()
    for d in range(1, n_dp):
        send(d, y).wait_send()


def in_vmem(count):
    return [pl.BlockSpec(memory_space=pltpu.VMEM)] * count


def make_table(n_dp, n_expert, feats, proj, rows):
    dma = pltpu.SemaphoreType.DMA
    near = 4 if n_expert % 4 == 0 else 1
    far = n_expert // near
    return pl.pallas_call(
        functools.partial(table_kernel, n_dp, n_expert),
        out_shape=(
            jax.ShapeDtypeStruct((n_expert, n_dp, feats.shape[0], proj.shape[2]), BF),
            jax.ShapeDtypeStruct(rows.shape, rows.dtype),
        ),
        in_specs=in_vmem(3),
        out_specs=tuple(in_vmem(2)),
        scratch_shapes=[
            pltpu.VMEM((n_expert,) + proj.shape[1:], BF),
            dma((n_expert,)),
            dma((n_expert,)),
            dma((n_expert,)),
            dma((n_expert,)),
            dma((n_dp,)),
            dma((n_dp,)),
            dma((far,)),
            dma((far,)),
            dma((far, near)),
            dma((far, near)),
        ],
        compiler_params=pltpu.CompilerParams(
            collective_id=0, has_side_effects=True, vmem_limit_bytes=48 * 2**20
        ),
    )(feats, proj, rows)


def share(n_dp, half):
    return pl.pallas_call(
        functools.partial(share_kernel, n_dp),
        out_shape=jax.ShapeDtypeStruct((n_dp,) + half.shape, half.dtype),
        in_specs=in_vmem(1),
        out_specs=in_vmem(1)[0],
        scratch_shapes=[pltpu.SemaphoreType.DMA((n_dp,)), pltpu.SemaphoreType.DMA((n_dp,))],
        compiler_params=pltpu.CompilerParams(
            collective_id=1, has_side_effects=True, vmem_limit_bytes=32 * 2**20
        ),
    )(half)


def body(
    cache,
    requests,
    routes,
    combine_weight,
    proj_weight,
    norm_gain,
    gate_weight,
    up_weight,
    down_weight,
    cotangent,
):
    width = cotangent.shape[1]
    n_expert = lax.axis_size("expert")
    experts = n_expert * gate_weight.shape[0]
    block = cache.shape[1]

    n_dp = lax.axis_size("dp")
    model_width = norm_gain.shape[0]

    token_row = (
        requests.reshape(-1)[:, None] * block + jnp.arange(block, dtype=jnp.int32)[None, :]
    ).reshape(-1)
    tokens = token_row.shape[0]
    capacity = max(2, 5 * tokens // (4 * experts))
    expert_id = routes[:, 0]
    order = jnp.arange(tokens, dtype=jnp.int32)
    earlier = (expert_id[:, None] == expert_id[None, :]) & (order[None, :] < order[:, None])
    slot_rank = jnp.sum(earlier.astype(jnp.int32), axis=1)
    position = expert_id * capacity + slot_rank
    hit = jnp.arange(experts * capacity, dtype=jnp.int32)[:, None] == position[None, :]
    pick = hit.astype(BF)
    slot_row = jnp.sum(jnp.where(hit, token_row[None, :] + 1, 0), axis=1) - 1

    token_weight = combine_weight[:, 0]
    scaled_grad = (token_weight[:, None] * cotangent.astype(F32)).astype(BF)
    sent = dot(pick, scaled_grad).astype(BF).reshape(experts, capacity, width)
    grad_rows = lax.all_to_all(sent, "expert", split_axis=0, concat_axis=0, tiled=True)
    grad_rows = grad_rows.reshape(-1, width)

    depth = proj_weight.shape[0]
    padded = -(-depth // 16) * 16
    groups = n_expert // n_dp
    lanes = width // groups
    feats = jnp.pad(
        cache.reshape(-1, n_expert, depth), ((0, 0), (0, 0), (0, padded - depth))
    ).reshape(-1, n_expert * padded)
    proj = jnp.pad(proj_weight, ((0, padded - depth), (0, 0)))
    proj = proj.reshape(padded, groups, lanes).transpose(1, 0, 2)
    ids = jnp.pad(slot_row.reshape(experts, 1, capacity), ((0, 0), (0, 7), (0, 128 - capacity)))
    blocks, got = make_table(n_dp, n_expert, feats, proj, ids)
    projected = blocks.transpose(1, 2, 0, 3).reshape(-1, model_width)
    values = projected.astype(F32)
    mean_square = jnp.mean(values * values, axis=1)
    table = (values * lax.rsqrt(mean_square + 1e-06)[:, None] * norm_gain[None, :]).astype(BF)
    table_rows = table.shape[0]
    rows = got[:, 0, :capacity].reshape(-1)
    select = (rows[:, None] == jnp.arange(table_rows, dtype=jnp.int32)[None, :]).astype(BF)

    gate_act = dot(table, gate_weight[0])
    up_act = dot(table, up_weight[0])
    half = (jax.nn.silu(gate_act) * up_act).astype(BF)
    halves = share(n_dp, half)
    hidden = halves.transpose(1, 0, 2).reshape(table_rows, -1)
    out_rows = dot(hidden, down_weight[0]).astype(BF)
    sent_out = dot(select, out_rows).astype(BF).reshape(-1, capacity, width)
    hidden_rows = dot(select, hidden).astype(BF)
    down_grad = dot(hidden_rows, grad_rows, ((0,), (0,))).astype(BF)
    returned = lax.all_to_all(sent_out, "expert", split_axis=0, concat_axis=0, tiled=True)
    token_out = dot(pick, returned.reshape(experts * capacity, width), ((0,), (0,)))
    mixed = (token_weight[:, None] * token_out).astype(BF)
    return mixed, down_grad[None]


def solution(mesh):
    return jax.shard_map(
        body,
        mesh=mesh,
        in_specs=(
            P("dp", None, None),
            P(None, "expert", None),
            P("expert", None),
            P("expert", None),
            P("expert", "dp"),
            P(),
            P("expert", None, "dp"),
            P("expert", None, "dp"),
            P("expert", None, "dp"),
            P("expert", "dp"),
        ),
        out_specs=(P("expert", "dp"), P("expert", None, "dp")),
        check_vma=False,
    )
```

```python
import functools

import jax
import jax.numpy as jnp
from jax import lax
from jax.experimental import pallas as pl
from jax.experimental.pallas import tpu as pltpu
from jax.sharding import PartitionSpec as P

MESH = pl.DeviceIdType.MESH

BF = jnp.bfloat16
F32 = jnp.float32


def dot(a, b, dims=((1,), (0,))):
    return lax.dot_general(a, b, (dims, ((), ())), preferred_element_type=F32)


def loop(start, stop, step):
    def run(i, carry):
        step(i)
        return carry

    lax.fori_loop(start, stop, run, 0)


def remote(src, dst, send_sem, recv_sem, device):
    return pltpu.make_async_remote_copy(
        src_ref=src,
        dst_ref=dst,
        send_sem=send_sem,
        recv_sem=recv_sem,
        device_id=device,
        device_id_type=MESH,
    )


def table_kernel(
    n_dp,
    n_expert,
    feat_ref,
    proj_ref,
    rows_ref,
    tab_ref,
    got_ref,
    held,
    proj_send,
    proj_recv,
    row_send,
    row_recv,
    dp_send,
    dp_recv,
    far_send,
    far_recv,
    near_send,
    near_recv,
):
    y = lax.axis_index("dp")
    e = lax.axis_index("expert")
    groups = n_expert // n_dp
    near = 4 if n_expert % 4 == 0 else 1
    far = n_expert // near
    a, b = e // near, e % near
    n = n_dp * n_expert
    me = y * n_expert + e
    other = ((y + 1) % n_dp, e)

    barrier = pltpu.get_barrier_semaphore()

    def greet(i):
        t = (me + i) % n
        pl.semaphore_signal(
            barrier, inc=1, device_id=(t // n_expert, t % n_expert), device_id_type=MESH
        )

    loop(1, n, greet)
    pl.semaphore_wait(barrier, n - 1)

    mine = e // groups == y

    lanes = held.shape[2]

    def group_of(j):
        if len(proj_ref.shape) == 3:
            return proj_ref.at[j]
        return proj_ref.at[:, pl.ds(pl.multiple_of(j * lanes, lanes), lanes)]

    def send_proj(dy, dj):
        j = (e + dj) % groups
        return remote(
            group_of(j),
            held.at[e],
            proj_send.at[dy * groups + dj],
            proj_recv.at[e],
            ((y + dy) % n_dp, y * groups + j),
        )

    for dj in range(groups):
        for dy in range(n_dp):
            if dy == 0 and dj == 0:
                pl.when(jnp.logical_not(mine))(lambda: send_proj(0, 0).start())
            else:
                send_proj(dy, dj).start()

    @pl.when(mine)
    def _():
        held[e] = group_of(e % groups)[...]

    got_ref[e] = rows_ref[e]

    def send_row(i):
        t = (e + i) % n_expert
        return remote(rows_ref.at[t], got_ref.at[e], row_send.at[i], row_recv.at[i], (y, t))

    loop(1, n_expert, lambda i: send_row(i).start())

    def await_proj(i):
        s = (e + i) % n_expert
        remote(held.at[s], held.at[s], proj_send.at[0], proj_recv.at[s], other).wait_recv()

    pl.when(jnp.logical_not(mine))(lambda: await_proj(0))
    loop(1, n_expert, await_proj)

    weight = held[...].reshape(-1, held.shape[2])
    part = jnp.dot(feat_ref[...], weight, preferred_element_type=jnp.float32)
    tab_ref[e, y] = part.astype(jnp.bfloat16)

    def over_dp(d, src):
        return remote(
            tab_ref.at[e, src],
            tab_ref.at[e, src],
            dp_send.at[d],
            dp_recv.at[d],
            ((y + d) % n_dp, e),
        )

    for d in range(1, n_dp):
        over_dp(d, y).start()
    for d in range(1, n_dp):
        over_dp(d, (y + n_dp - d) % n_dp).wait_recv()

    def to_far(d, block):
        return remote(
            tab_ref.at[block],
            tab_ref.at[block],
            far_send.at[d],
            far_recv.at[d],
            (y, (a + d) % far * near + b),
        )

    p, q = b // 2, b % 2

    def at(d, x, core):
        return (a + far - d) % far * near + x * 2 + core

    def to_near(d, c, block):
        x, core = (1 - p, q) if c == 0 else (p, 1 - q)
        return remote(
            tab_ref.at[block],
            tab_ref.at[block],
            near_send.at[d, c],
            near_recv.at[d, c],
            (y, a * near + x * 2 + core),
        )

    for d in range(1, far):
        to_far(d, e).start()
    for d in range(far + 1):
        if d < far:
            block = (a + far - d) % far * near + b
            if d:
                to_far(d, block).wait_recv()
            if near == 4:
                to_near(d, 0, block).start()
                to_near(d, 1, block).start()
        if d and near == 4:
            to_near(d - 1, 0, at(d - 1, 1 - p, q)).wait_recv()
            to_near(d - 1, 2, at(d - 1, 1 - p, q)).start()
    if near == 4:
        for d in range(far):
            to_near(d, 1, at(d, p, 1 - q)).wait_recv()
            to_near(d, 2, at(d, 1 - p, 1 - q)).wait_recv()

    def await_row(i):
        s = (e + n_expert - i) % n_expert
        remote(
            rows_ref.at[0], got_ref.at[s], row_send.at[i], row_recv.at[i], other
        ).wait_recv()

    loop(1, n_expert, await_row)
    pl.when(jnp.logical_not(mine))(lambda: send_proj(0, 0).wait_send())
    for dj in range(groups):
        for dy in range(n_dp):
            if dy or dj:
                send_proj(dy, dj).wait_send()
    loop(1, n_expert, lambda i: send_row(i).wait_send())
    for d in range(1, n_dp):
        over_dp(d, y).wait_send()
    for d in range(1, far):
        to_far(d, e).wait_send()
    if near == 4:
        for d in range(far):
            to_near(d, 0, at(d, p, q)).wait_send()
            to_near(d, 1, at(d, p, q)).wait_send()
            to_near(d, 2, at(d, 1 - p, q)).wait_send()


def share_kernel(n_dp, half_ref, out_ref, send_sem, recv_sem):
    y = lax.axis_index("dp")
    e = lax.axis_index("expert")
    barrier = pltpu.get_barrier_semaphore()
    for d in range(1, n_dp):
        pl.semaphore_signal(
            barrier, inc=1, device_id=((y + d) % n_dp, e), device_id_type=MESH
        )
    pl.semaphore_wait(barrier, n_dp - 1)

    def send(d, src):
        return remote(
            half_ref, out_ref.at[src], send_sem.at[d], recv_sem.at[d], ((y + d) % n_dp, e)
        )

    for d in range(1, n_dp):
        send(d, y).start()
    out_ref[y] = half_ref[...]
    for d in range(1, n_dp):
        send(d, (y + n_dp - d) % n_dp).wait_recv()
    for d in range(1, n_dp):
        send(d, y).wait_send()


def in_vmem(count):
    return [pl.BlockSpec(memory_space=pltpu.VMEM)] * count


def make_table(n_dp, n_expert, lanes, feats, proj, rows):
    dma = pltpu.SemaphoreType.DMA
    near = 4 if n_expert % 4 == 0 else 1
    far = n_expert // near
    return pl.pallas_call(
        functools.partial(table_kernel, n_dp, n_expert),
        out_shape=(
            jax.ShapeDtypeStruct((n_expert, n_dp, feats.shape[0], lanes), BF),
            jax.ShapeDtypeStruct(rows.shape, rows.dtype),
        ),
        in_specs=in_vmem(3),
        out_specs=tuple(in_vmem(2)),
        scratch_shapes=[
            pltpu.VMEM((n_expert, proj.shape[-2], lanes), BF),
            dma((n_expert,)),
            dma((n_expert,)),
            dma((n_expert,)),
            dma((n_expert,)),
            dma((n_dp,)),
            dma((n_dp,)),
            dma((far,)),
            dma((far,)),
            dma((far, near)),
            dma((far, near)),
        ],
        compiler_params=pltpu.CompilerParams(
            collective_id=0, has_side_effects=True, vmem_limit_bytes=48 * 2**20
        ),
    )(feats, proj, rows)


def share(n_dp, half):
    return pl.pallas_call(
        functools.partial(share_kernel, n_dp),
        out_shape=jax.ShapeDtypeStruct((n_dp,) + half.shape, half.dtype),
        in_specs=in_vmem(1),
        out_specs=in_vmem(1)[0],
        scratch_shapes=[pltpu.SemaphoreType.DMA((n_dp,)), pltpu.SemaphoreType.DMA((n_dp,))],
        compiler_params=pltpu.CompilerParams(
            collective_id=1, has_side_effects=True, vmem_limit_bytes=32 * 2**20
        ),
    )(half)


def body(
    cache,
    requests,
    routes,
    combine_weight,
    proj_weight,
    norm_gain,
    gate_weight,
    up_weight,
    down_weight,
    cotangent,
):
    width = cotangent.shape[1]
    n_expert = lax.axis_size("expert")
    experts = n_expert * gate_weight.shape[0]
    block = cache.shape[1]

    n_dp = lax.axis_size("dp")
    model_width = norm_gain.shape[0]

    token_row = (
        requests.reshape(-1)[:, None] * block + jnp.arange(block, dtype=jnp.int32)[None, :]
    ).reshape(-1)
    tokens = token_row.shape[0]
    capacity = max(2, 5 * tokens // (4 * experts))
    expert_id = routes[:, 0]
    order = jnp.arange(tokens, dtype=jnp.int32)
    earlier = (expert_id[:, None] == expert_id[None, :]) & (order[None, :] < order[:, None])
    slot_rank = jnp.sum(earlier.astype(jnp.int32), axis=1)
    position = expert_id * capacity + slot_rank
    hit = jnp.arange(experts * capacity, dtype=jnp.int32)[:, None] == position[None, :]
    pick = hit.astype(BF)
    slot_row = jnp.sum(jnp.where(hit, token_row[None, :] + 1, 0), axis=1) - 1

    token_weight = combine_weight[:, 0]
    scaled_grad = (token_weight[:, None] * cotangent.astype(F32)).astype(BF)
    sent = dot(pick, scaled_grad).astype(BF).reshape(experts, capacity, width)
    depth = proj_weight.shape[0]
    padded = -(-depth // 16) * 16
    groups = n_expert // n_dp
    lanes = width // groups
    spot = jnp.arange(n_expert * padded, dtype=jnp.int32)
    origin = jnp.where(spot % padded < depth, spot // padded * depth + spot % padded, -1)
    source = jnp.arange(n_expert * depth, dtype=jnp.int32)
    spread = (source[:, None] == origin[None, :]).astype(BF)
    feats = dot(cache.reshape(-1, n_expert * depth), spread).astype(BF)
    proj = jnp.pad(proj_weight, ((0, padded - depth), (0, 0)))
    if lanes % 128:
        proj = proj.reshape(padded, groups, lanes).transpose(1, 0, 2)
    ids = jnp.pad(slot_row.reshape(experts, 1, capacity), ((0, 0), (0, 7), (0, 128 - capacity)))
    blocks, got = make_table(n_dp, n_expert, lanes, feats, proj, ids)
    sent, got = lax.optimization_barrier((sent, got))
    grad_rows = lax.all_to_all(sent, "expert", split_axis=0, concat_axis=0, tiled=True)
    grad_rows = grad_rows.reshape(-1, width)
    projected = blocks.transpose(1, 2, 0, 3).reshape(-1, model_width)
    values = projected.astype(F32)
    mean_square = jnp.mean(values * values, axis=1)
    table = (values * lax.rsqrt(mean_square + 1e-06)[:, None] * norm_gain[None, :]).astype(BF)
    table_rows = table.shape[0]
    rows = got[:, 0, :capacity].reshape(-1)
    select = (rows[:, None] == jnp.arange(table_rows, dtype=jnp.int32)[None, :]).astype(BF)

    gate_act = dot(table, gate_weight[0])
    up_act = dot(table, up_weight[0])
    half = (jax.nn.silu(gate_act) * up_act).astype(BF)
    halves = share(n_dp, half)
    down = down_weight[0].reshape(n_dp, half.shape[1], width)
    out_rows = dot(halves, down, ((0, 2), (0, 1))).astype(BF)
    sent_out = dot(select, out_rows).astype(BF).reshape(-1, capacity, width)
    down_grad = [
        dot(dot(select, halves[i]).astype(BF), grad_rows, ((0,), (0,))).astype(BF)
        for i in range(n_dp)
    ]
    down_grad = jnp.concatenate(down_grad, axis=0)
    returned = lax.all_to_all(sent_out, "expert", split_axis=0, concat_axis=0, tiled=True)
    token_out = dot(pick, returned.reshape(experts * capacity, width), ((0,), (0,)))
    mixed = (token_weight[:, None] * token_out).astype(BF)
    return mixed, down_grad[None]


def solution(mesh):
    return jax.shard_map(
        body,
        mesh=mesh,
        in_specs=(
            P("dp", None, None),
            P(None, "expert", None),
            P("expert", None),
            P("expert", None),
            P("expert", "dp"),
            P(),
            P("expert", None, "dp"),
            P("expert", None, "dp"),
            P("expert", None, "dp"),
            P("expert", "dp"),
        ),
        out_specs=(P("expert", "dp"), P("expert", None, "dp")),
        check_vma=False,
    )
```

```python
import functools

import jax
import jax.numpy as jnp
from jax import lax
from jax.experimental import pallas as pl
from jax.experimental.pallas import tpu as pltpu
from jax.sharding import PartitionSpec as P

MESH = pl.DeviceIdType.MESH

BF = jnp.bfloat16
F32 = jnp.float32


def dot(a, b, dims=((1,), (0,))):
    return lax.dot_general(a, b, (dims, ((), ())), preferred_element_type=F32)


def loop(start, stop, step):
    def run(i, carry):
        step(i)
        return carry

    lax.fori_loop(start, stop, run, 0)


def remote(src, dst, send_sem, recv_sem, device):
    return pltpu.make_async_remote_copy(
        src_ref=src,
        dst_ref=dst,
        send_sem=send_sem,
        recv_sem=recv_sem,
        device_id=device,
        device_id_type=MESH,
    )


def table_kernel(
    n_dp,
    n_expert,
    feat_ref,
    proj_ref,
    rows_ref,
    tab_ref,
    got_ref,
    held,
    proj_send,
    proj_recv,
    pass_send,
    row_send,
    row_recv,
    dp_send,
    dp_recv,
    far_send,
    far_recv,
    near_send,
    near_recv,
):
    y = lax.axis_index("dp")
    e = lax.axis_index("expert")
    groups = n_expert // n_dp
    near = 4 if n_expert % 4 == 0 else 1
    far = n_expert // near
    a, b = e // near, e % near
    n = n_dp * n_expert
    me = y * n_expert + e
    other = ((y + 1) % n_dp, e)

    barrier = pltpu.get_barrier_semaphore()

    def greet(i):
        t = (me + i) % n
        pl.semaphore_signal(
            barrier, inc=1, device_id=(t // n_expert, t % n_expert), device_id_type=MESH
        )

    loop(1, n, greet)
    pl.semaphore_wait(barrier, n - 1)

    mine = e // groups == y

    lanes = held.shape[2]

    def group_of(j):
        if len(proj_ref.shape) == 3:
            return proj_ref.at[j]
        return proj_ref.at[:, pl.ds(pl.multiple_of(j * lanes, lanes), lanes)]

    def send_proj(dj):
        j = (e + dj) % groups
        return remote(
            group_of(j), held.at[e], proj_send.at[dj], proj_recv.at[e], (y, y * groups + j)
        )

    pl.when(jnp.logical_not(mine))(lambda: send_proj(0).start())
    for dj in range(1, groups):
        send_proj(dj).start()

    got_ref[e] = rows_ref[e]

    def send_row(i):
        t = (e + i) % n_expert
        return remote(rows_ref.at[t], got_ref.at[e], row_send.at[i], row_recv.at[i], (y, t))

    loop(1, n_expert, lambda i: send_row(i).start())

    def await_proj(i):
        s = (e + n_expert - i) % n_expert
        remote(held.at[s], held.at[s], proj_send.at[0], proj_recv.at[s], other).wait_recv()

    def pass_on(i, d):
        s = (e + n_expert - i) % n_expert
        return remote(
            held.at[s], held.at[s], pass_send.at[d, i], proj_recv.at[s], ((y + d) % n_dp, e)
        )

    @pl.when(mine)
    def _():
        held[e] = group_of(e % groups)[...]

        def relay(i):
            for d in range(1, n_dp):
                pass_on(i, d).start()

        relay(0)

        def step(i):
            await_proj(i)
            relay(i)

        loop(1, n_expert, step)

    pl.when(jnp.logical_not(mine))(lambda: loop(0, n_expert, await_proj))

    weight = held[...].reshape(-1, held.shape[2])
    part = jnp.dot(feat_ref[...], weight, preferred_element_type=jnp.float32)
    tab_ref[e, y] = part.astype(jnp.bfloat16)

    def over_dp(d, src):
        return remote(
            tab_ref.at[e, src],
            tab_ref.at[e, src],
            dp_send.at[d],
            dp_recv.at[d],
            ((y + d) % n_dp, e),
        )

    for d in range(1, n_dp):
        over_dp(d, y).start()
    for d in range(1, n_dp):
        over_dp(d, (y + n_dp - d) % n_dp).wait_recv()

    def to_far(d, block):
        return remote(
            tab_ref.at[block],
            tab_ref.at[block],
            far_send.at[d],
            far_recv.at[d],
            (y, (a + d) % far * near + b),
        )

    p, q = b // 2, b % 2

    def at(d, x, core):
        return (a + far - d) % far * near + x * 2 + core

    def to_near(d, c, block):
        x, core = (1 - p, q) if c == 0 else (p, 1 - q)
        return remote(
            tab_ref.at[block],
            tab_ref.at[block],
            near_send.at[d, c],
            near_recv.at[d, c],
            (y, a * near + x * 2 + core),
        )

    for d in range(1, far):
        to_far(d, e).start()
    for d in range(far + 1):
        if d < far:
            block = (a + far - d) % far * near + b
            if d:
                to_far(d, block).wait_recv()
            if near == 4:
                to_near(d, 0, block).start()
                to_near(d, 1, block).start()
        if d and near == 4:
            to_near(d - 1, 0, at(d - 1, 1 - p, q)).wait_recv()
            to_near(d - 1, 2, at(d - 1, 1 - p, q)).start()
    if near == 4:
        for d in range(far):
            to_near(d, 1, at(d, p, 1 - q)).wait_recv()
            to_near(d, 2, at(d, 1 - p, 1 - q)).wait_recv()

    def await_row(i):
        s = (e + n_expert - i) % n_expert
        remote(
            rows_ref.at[0], got_ref.at[s], row_send.at[i], row_recv.at[i], other
        ).wait_recv()

    loop(1, n_expert, await_row)
    pl.when(jnp.logical_not(mine))(lambda: send_proj(0).wait_send())
    for dj in range(1, groups):
        send_proj(dj).wait_send()

    @pl.when(mine)
    def _():
        def sent(i):
            for d in range(1, n_dp):
                pass_on(i, d).wait_send()

        loop(0, n_expert, sent)

    loop(1, n_expert, lambda i: send_row(i).wait_send())
    for d in range(1, n_dp):
        over_dp(d, y).wait_send()
    for d in range(1, far):
        to_far(d, e).wait_send()
    if near == 4:
        for d in range(far):
            to_near(d, 0, at(d, p, q)).wait_send()
            to_near(d, 1, at(d, p, q)).wait_send()
            to_near(d, 2, at(d, 1 - p, q)).wait_send()


def share_kernel(n_dp, half_ref, out_ref, send_sem, recv_sem):
    y = lax.axis_index("dp")
    e = lax.axis_index("expert")
    barrier = pltpu.get_barrier_semaphore()
    for d in range(1, n_dp):
        pl.semaphore_signal(
            barrier, inc=1, device_id=((y + d) % n_dp, e), device_id_type=MESH
        )
    pl.semaphore_wait(barrier, n_dp - 1)

    def send(d, src):
        return remote(
            half_ref, out_ref.at[src], send_sem.at[d], recv_sem.at[d], ((y + d) % n_dp, e)
        )

    for d in range(1, n_dp):
        send(d, y).start()
    out_ref[y] = half_ref[...]
    for d in range(1, n_dp):
        send(d, (y + n_dp - d) % n_dp).wait_recv()
    for d in range(1, n_dp):
        send(d, y).wait_send()


def in_vmem(count):
    return [pl.BlockSpec(memory_space=pltpu.VMEM)] * count


def make_table(n_dp, n_expert, lanes, feats, proj, rows):
    dma = pltpu.SemaphoreType.DMA
    near = 4 if n_expert % 4 == 0 else 1
    far = n_expert // near
    return pl.pallas_call(
        functools.partial(table_kernel, n_dp, n_expert),
        out_shape=(
            jax.ShapeDtypeStruct((n_expert, n_dp, feats.shape[0], lanes), BF),
            jax.ShapeDtypeStruct(rows.shape, rows.dtype),
        ),
        in_specs=in_vmem(3),
        out_specs=tuple(in_vmem(2)),
        scratch_shapes=[
            pltpu.VMEM((n_expert, proj.shape[-2], lanes), BF),
            dma((n_expert,)),
            dma((n_expert,)),
            dma((n_dp, n_expert)),
            dma((n_expert,)),
            dma((n_expert,)),
            dma((n_dp,)),
            dma((n_dp,)),
            dma((far,)),
            dma((far,)),
            dma((far, near)),
            dma((far, near)),
        ],
        compiler_params=pltpu.CompilerParams(
            collective_id=0, has_side_effects=True, vmem_limit_bytes=48 * 2**20
        ),
    )(feats, proj, rows)


def share(n_dp, half):
    return pl.pallas_call(
        functools.partial(share_kernel, n_dp),
        out_shape=jax.ShapeDtypeStruct((n_dp,) + half.shape, half.dtype),
        in_specs=in_vmem(1),
        out_specs=in_vmem(1)[0],
        scratch_shapes=[pltpu.SemaphoreType.DMA((n_dp,)), pltpu.SemaphoreType.DMA((n_dp,))],
        compiler_params=pltpu.CompilerParams(
            collective_id=1, has_side_effects=True, vmem_limit_bytes=32 * 2**20
        ),
    )(half)


def body(
    cache,
    requests,
    routes,
    combine_weight,
    proj_weight,
    norm_gain,
    gate_weight,
    up_weight,
    down_weight,
    cotangent,
):
    width = cotangent.shape[1]
    n_expert = lax.axis_size("expert")
    experts = n_expert * gate_weight.shape[0]
    block = cache.shape[1]

    n_dp = lax.axis_size("dp")
    model_width = norm_gain.shape[0]

    token_row = (
        requests.reshape(-1)[:, None] * block + jnp.arange(block, dtype=jnp.int32)[None, :]
    ).reshape(-1)
    tokens = token_row.shape[0]
    capacity = max(2, 5 * tokens // (4 * experts))
    expert_id = routes[:, 0]
    order = jnp.arange(tokens, dtype=jnp.int32)
    earlier = (expert_id[:, None] == expert_id[None, :]) & (order[None, :] < order[:, None])
    slot_rank = jnp.sum(earlier.astype(jnp.int32), axis=1)
    position = expert_id * capacity + slot_rank
    hit = jnp.arange(experts * capacity, dtype=jnp.int32)[:, None] == position[None, :]
    pick = hit.astype(BF)
    slot_row = jnp.sum(jnp.where(hit, token_row[None, :] + 1, 0), axis=1) - 1

    token_weight = combine_weight[:, 0]
    scaled_grad = (token_weight[:, None] * cotangent.astype(F32)).astype(BF)
    sent = dot(pick, scaled_grad).astype(BF).reshape(experts, capacity, width)
    depth = proj_weight.shape[0]
    padded = -(-depth // 16) * 16
    groups = n_expert // n_dp
    lanes = width // groups
    spot = jnp.arange(n_expert * padded, dtype=jnp.int32)
    origin = jnp.where(spot % padded < depth, spot // padded * depth + spot % padded, -1)
    source = jnp.arange(n_expert * depth, dtype=jnp.int32)
    spread = (source[:, None] == origin[None, :]).astype(BF)
    feats = dot(cache.reshape(-1, n_expert * depth), spread).astype(BF)
    proj = jnp.pad(proj_weight, ((0, padded - depth), (0, 0)))
    if lanes % 128:
        proj = proj.reshape(padded, groups, lanes).transpose(1, 0, 2)
    ids = jnp.pad(slot_row.reshape(experts, 1, capacity), ((0, 0), (0, 7), (0, 128 - capacity)))
    blocks, got = make_table(n_dp, n_expert, lanes, feats, proj, ids)
    sent, got = lax.optimization_barrier((sent, got))
    grad_rows = lax.all_to_all(sent, "expert", split_axis=0, concat_axis=0, tiled=True)
    grad_rows = grad_rows.reshape(-1, width)
    projected = blocks.transpose(1, 2, 0, 3).reshape(-1, model_width)
    values = projected.astype(F32)
    mean_square = jnp.mean(values * values, axis=1)
    table = (values * lax.rsqrt(mean_square + 1e-06)[:, None] * norm_gain[None, :]).astype(BF)
    table_rows = table.shape[0]
    rows = got[:, 0, :capacity].reshape(-1)
    select = (rows[:, None] == jnp.arange(table_rows, dtype=jnp.int32)[None, :]).astype(BF)

    gate_act = dot(table, gate_weight[0])
    up_act = dot(table, up_weight[0])
    half = (jax.nn.silu(gate_act) * up_act).astype(BF)
    halves, grad_rows = lax.optimization_barrier((share(n_dp, half), grad_rows))
    down = down_weight[0].reshape(n_dp, half.shape[1], width)
    out_rows = dot(halves, down, ((0, 2), (0, 1))).astype(BF)
    sent_out = dot(select, out_rows).astype(BF).reshape(-1, capacity, width)
    hidden_rows = jnp.concatenate(
        [dot(select, halves[i]).astype(BF) for i in range(n_dp)], axis=1
    )
    down_grad = dot(hidden_rows, grad_rows, ((0,), (0,))).astype(BF)
    returned = lax.all_to_all(sent_out, "expert", split_axis=0, concat_axis=0, tiled=True)
    token_out = dot(pick, returned.reshape(experts * capacity, width), ((0,), (0,)))
    mixed = (token_weight[:, None] * token_out).astype(BF)
    return mixed, down_grad[None]


def solution(mesh):
    return jax.shard_map(
        body,
        mesh=mesh,
        in_specs=(
            P("dp", None, None),
            P(None, "expert", None),
            P("expert", None),
            P("expert", None),
            P("expert", "dp"),
            P(),
            P("expert", None, "dp"),
            P("expert", None, "dp"),
            P("expert", None, "dp"),
            P("expert", "dp"),
        ),
        out_specs=(P("expert", "dp"), P("expert", None, "dp")),
        check_vma=False,
    )
```
